32 devices in a mesh: ctx: 8 (over z, core), ch: 4 (over y, x).
Axes of the slice: x: 2, y: 2, z: 4, core: 2. Of those that a mesh axis runs over, the one named last changes fastest.
Arguments:
- signal: bfloat16 [1024, 8192], P('ctx', 'ch'), may hold values from -170 to 170, as said below
- norm_gain: float32 [8192], P('ch'), may hold values from 0.1 to 1.9
- skip_gain: float32 [8192], P('ch'), may hold values from 0.5 to 1.5
- filter_taps: bfloat16 [1024, 8192], P('ctx', 'ch'), may hold values from -1.5 to 1.5, as said below
- out_gate: bfloat16 [1024, 8192], P('ctx', 'ch'), may hold values from -6 to 6
Outputs:
- mixture: bfloat16 [1024, 8192], P('ctx', 'ch')
The draws below stay inside these ranges and needn't reach their ends.
Inputs may be any that keep to these rules, and one draw needn't show every extreme that they name: `signal`: features whose channels and tokens have different scales. `filter_taps`: a filter whose taps fall off along the lags at a rate that differs between channels.
All inputs are finite; a program needn't handle non-finite values.
Results may differ from the reference program's by a relative error of at most 0.006.
Values may be sent and summed in bfloat16 or wider, within the bound.
No kernel may reach another device: no remote copies, remote signals or barrier semaphores. Data moves between devices by JAX's collectives and lax.ppermute only.
A program may use at most 64 MiB of HBM per device.

```python
import math
import jax
import jax.numpy as jnp
from jax import lax

C = 8192
LENGTH = 1024


def draw_signal(key, part):
    noise_key = jax.random.fold_in(key, 3)
    row_key = jax.random.fold_in(key, 5)
    noise_draw = jnp.clip(jax.random.normal(noise_key, (LENGTH, C), jnp.float32), -5.0, 5.0)
    column = jnp.exp(math.log(10.0) * jnp.arange(C, dtype=jnp.float32) / C) / 3.0
    row_scale = jnp.exp(jax.random.uniform(row_key, (LENGTH, 1), jnp.float32, 0.0, math.log(10.0)))
    return (noise_draw * row_scale * column[None, :]).astype(jnp.bfloat16)


def draw_filter_taps(key, part):
    decay_key = jax.random.fold_in(key, 7)
    noise_key = jax.random.fold_in(key, 11)
    longest = math.log(32.0 * LENGTH)
    log_decay = jax.random.uniform(decay_key, (C,), jnp.float32, math.log(30.0), longest)
    noise_draw = jnp.clip(jax.random.normal(noise_key, (LENGTH, C), jnp.float32), -5.0, 5.0)
    decay_len = jnp.exp(log_decay)
    lag_pos = jnp.arange(LENGTH, dtype=jnp.float32)
    amplitude = 1.0 / jnp.sqrt(0.5 * jnp.minimum(decay_len, 2.0 * LENGTH))
    return (noise_draw * jnp.exp(-lag_pos[:, None] / decay_len[None, :]) * amplitude[None, :]).astype(jnp.bfloat16)


def steps_of(stream_key, dims, pieces, smallest, largest):
    gain, own = 1.0, jax.random.fold_in(stream_key, 6)
    for position, shards_of in pieces:
        draws = jnp.exp(jax.random.uniform(jax.random.fold_in(own, position), (shards_of,), jnp.float32, smallest / len(pieces), largest / len(pieces)))
        gain = gain * jnp.repeat(draws, dims[position] // shards_of).reshape([-1 if axis == position else 1 for axis in range(len(dims))])
    return gain


def scatter_about(key, shape, width, limit, cuts=(), kind=jnp.bfloat16):
    entries = jax.random.normal(key, shape, jnp.float32) * width
    if len(cuts) > 0:
        entries = steps_of(key, shape, cuts, -0.22, 0.18) * entries
    return jnp.clip(entries, min=-limit, max=limit).astype(kind)


def setup_inputs(seed: int = 0) -> dict:
    key_list = jax.random.split(jax.random.key(seed), 6)
    signal = draw_signal(jax.random.fold_in(key_list[5], 71), 0)
    norm_gain = jnp.clip(1.0 + 0.18 * jax.random.normal(key_list[1], (C,), jnp.float32), 0.1, 1.9)
    skip_gain = jnp.clip(0.5 + 1.0 * jax.random.uniform(key_list[2], (C,), jnp.float32) ** steps_of(key_list[2], (C,), ((0, 4),), -0.2, 0.2), 0.5, 1.5)
    filter_taps = draw_filter_taps(jax.random.fold_in(key_list[5], 71), 0)
    out_gate = scatter_about(key_list[4], (LENGTH, C), 1.0, 6.0, ((0, 8), (1, 4)))
    return dict(signal=signal, norm_gain=norm_gain, skip_gain=skip_gain, filter_taps=filter_taps, out_gate=out_gate)


EPS = 1e-06

def reference(signal, norm_gain, skip_gain, filter_taps, out_gate):
    values = signal.astype(jnp.float32)
    row_power = lax.optimization_barrier(jnp.mean(values * values, axis=1, keepdims=True))
    normed = (values * lax.rsqrt(row_power + EPS) * norm_gain[None, :]).astype(jnp.bfloat16)
    seq_len = normed.shape[0]
    padded_len = 2 * seq_len
    group_width = 256
    group_count = C // group_width
    signal_groups = normed.astype(jnp.float32).reshape(seq_len, group_count, group_width).transpose(1, 0, 2)
    filter_groups = filter_taps.astype(jnp.float32).reshape(seq_len, group_count, group_width).transpose(1, 0, 2)

    def convolve_group(inputs_pair):
        sig_group, fil_group = inputs_pair
        product = jnp.fft.rfft(sig_group, n=padded_len, axis=0) * jnp.fft.rfft(fil_group, n=padded_len, axis=0)
        return jnp.fft.irfft(product, n=padded_len, axis=0)[:seq_len]
    convolved = lax.map(convolve_group, (signal_groups, filter_groups))
    convolved = convolved.transpose(1, 0, 2).reshape(seq_len, C)
    mixture = out_gate.astype(jnp.float32) * (convolved + skip_gain[None, :] * normed.astype(jnp.float32))
    return mixture.astype(jnp.bfloat16)
```

```python
import functools
import math

import jax
import jax.numpy as jnp
import numpy as np
from jax import lax
from jax.experimental import pallas as pl
from jax.experimental.pallas import tpu as pltpu
from jax.sharding import PartitionSpec as P

C = 8192

EPS = 1e-06

VMEM = pl.BlockSpec(memory_space=pltpu.VMEM)
SMEM = pl.BlockSpec(memory_space=pltpu.SMEM)


def row_angles(block):
    order = np.concatenate([np.arange(0, block, 2), np.arange(1, block, 2)])
    tokens = np.arange(block)
    turns = (2 * order[:, None] + 1) * tokens[None, :] % (4 * block)
    return turns * (math.pi / (2 * block))


def two_parts(table):
    table = table.astype(np.float32)
    high = table.astype(jnp.bfloat16)
    low = (table - high.astype(np.float32)).astype(jnp.bfloat16)
    return jnp.asarray(high), jnp.asarray(low)


def forward_tables(block):
    angles = row_angles(block)
    return two_parts(np.concatenate([np.cos(angles), -np.sin(angles)]))


def inverse_tables(block):
    angles = row_angles(block).T
    return two_parts(np.concatenate([np.cos(angles), -np.sin(angles)], axis=1) / block)


def transform_blocks(chips, place_ref, blocks, high_ref, low_ref, whole, spectra):
    z, core = place_ref[0], place_ref[1]
    rows = whole.shape[1] // 2
    for distance in range(chips):
        own, other = blocks[2 * distance], blocks[2 * distance + 1]
        whole[distance, pl.ds(pl.multiple_of(core * rows, rows), rows), :] = own[...]
        whole[distance, pl.ds(pl.multiple_of((1 - core) * rows, rows), rows), :] = other[...]
        block = whole[distance]
        spectrum = jnp.dot(high_ref[...], block, preferred_element_type=jnp.float32)
        spectrum += jnp.dot(low_ref[...], block, preferred_element_type=jnp.float32)
        spectra[lax.rem(z - distance + chips, chips)] = spectrum


def filter_kernel(chips, place_ref, high_ref, low_ref, *rest):
    blocks, (out_ref, whole) = rest[: 2 * chips], rest[2 * chips :]
    transform_blocks(chips, place_ref, blocks, high_ref, low_ref, whole, out_ref)
    block = whole.shape[1]
    half = block // 2
    parts = [pl.ds(i * half, half) for i in range(4)]
    re_even, re_odd, im_even, im_odd = parts
    for lag in range(chips - 1, 0, -1):
        out_ref[lag, re_even, :] -= out_ref[lag - 1, im_even, :]
        out_ref[lag, im_even, :] += out_ref[lag - 1, re_even, :]
        out_ref[lag, re_odd, :] += out_ref[lag - 1, im_odd, :]
        out_ref[lag, im_odd, :] -= out_ref[lag - 1, re_odd, :]


def signal_kernel(chips, place_ref, fil_ref, high_ref, low_ref, inv_ref, *rest):
    blocks, outs = rest[: 2 * chips], rest[2 * chips : 3 * chips]
    whole, spectra, products = rest[3 * chips :]
    transform_blocks(chips, place_ref, blocks, high_ref, low_ref, whole, spectra)
    _, block, columns = whole.shape
    tile, lanes = 16, min(columns, 128)

    @pl.loop(0, block // tile)
    def _(step):
        start = pl.multiple_of(step * tile, tile)
        re_rows, im_rows = pl.ds(start, tile), pl.ds(block + start, tile)
        for first in range(0, columns, lanes):
            cut = pl.ds(first, lanes)
            for target in range(chips):
                sum_re = sum_im = None
                for source in range(target + 1):
                    sig_re, sig_im = spectra[source, re_rows, cut], spectra[source, im_rows, cut]
                    fil_re = fil_ref[target - source, re_rows, cut]
                    fil_im = fil_ref[target - source, im_rows, cut]
                    re = sig_re * fil_re - sig_im * fil_im
                    im = sig_re * fil_im + sig_im * fil_re
                    sum_re = re if sum_re is None else sum_re + re
                    sum_im = im if sum_im is None else sum_im + im
                products[target, re_rows, cut] = sum_re.astype(jnp.bfloat16)
                products[target, im_rows, cut] = sum_im.astype(jnp.bfloat16)

    z = place_ref[0]
    for distance in range(chips):
        target = lax.rem(z + distance, chips)
        result = jnp.dot(inv_ref[...], products[target], preferred_element_type=jnp.float32)
        outs[distance][...] = result.astype(jnp.bfloat16)


def mix_kernel(chips, place_ref, normed_ref, gate_ref, skip_ref, *rest):
    pieces, out_ref = rest[: 2 * chips], rest[2 * chips]
    z, core = place_ref[0], place_ref[1]
    rows = out_ref.shape[0]
    mine = pieces[0].shape[1]
    for distance in range(chips):
        source = lax.rem(z - distance + chips, chips)
        own = pieces[2 * distance][pl.ds(pl.multiple_of(core * rows, rows), rows), :]
        other = pieces[2 * distance + 1][...]
        for owner, conv in ((core, own), (1 - core, other)):
            cut = pl.ds(pl.multiple_of((2 * source + owner) * mine, mine), mine)
            direct = skip_ref[:, cut] * normed_ref[:, cut].astype(jnp.float32)
            mixed = gate_ref[:, cut].astype(jnp.float32) * (conv.astype(jnp.float32) + direct)
            out_ref[:, cut] = mixed.astype(jnp.bfloat16)


def mix_plain(chips, z, core, normed, gate, skip, pieces):
    rows, channels = normed.shape
    mine = channels // (2 * chips)
    convolved = jnp.zeros((rows, channels), jnp.bfloat16)
    for distance in range(chips):
        source = lax.rem(z - distance + chips, chips)
        own = lax.dynamic_slice_in_dim(pieces[2 * distance], core * rows, rows, 0)
        for owner, conv in ((core, own), (1 - core, pieces[2 * distance + 1])):
            first = (2 * source + owner) * mine
            convolved = lax.dynamic_update_slice_in_dim(convolved, conv, first, 1)
    direct = skip * normed.astype(jnp.float32)
    return (gate.astype(jnp.float32) * (convolved.astype(jnp.float32) + direct)).astype(
        jnp.bfloat16
    )


def cost(flops):
    return pl.CostEstimate(flops=flops, bytes_accessed=4 * 1024 * 1024, transcendentals=0)


def along_chips(piece, distance):
    count = lax.axis_size("ctx")
    return lax.ppermute(piece, "ctx", [(i, (i + 2 * distance) % count) for i in range(count)])


def other_core(piece):
    return lax.ppermute(piece, "ctx", [(i, i ^ 1) for i in range(lax.axis_size("ctx"))])


def sum_over(values, axis):
    count = lax.axis_size(axis)
    if count & (count - 1):
        return lax.psum(values, axis)
    step = 1
    while step < count:
        values = values + lax.ppermute(values, axis, [(i, i ^ step) for i in range(count)])
        step *= 2
    return values


def distances(chips):
    return sorted(range(1, chips), key=lambda d: -min(d, chips - d))


def after(value, earlier):
    return lax.optimization_barrier((value, earlier))[0]


def cut_for_chips(array, z, chips):
    width = array.shape[1] // chips
    return [
        lax.dynamic_slice_in_dim(array, lax.rem(z + distance, chips) * width, width, 1)
        for distance in range(chips)
    ]


def gather_tokens(pieces, core, chips, ready=None):
    mine = pieces[0].shape[1] // 2
    pieces = list(pieces)
    for distance in distances(chips):
        pieces[distance] = along_chips(pieces[distance], distance)
    if ready is not None:
        pieces = after(pieces, ready(pieces))
    blocks = []
    for distance in range(chips):
        piece = pieces[distance]
        blocks.append(lax.dynamic_slice_in_dim(piece, core * mine, mine, 1))
        blocks.append(other_core(lax.dynamic_slice_in_dim(piece, (1 - core) * mine, mine, 1)))
    return blocks


def local(signal, norm_gain, skip_gain, filter_taps, out_gate):
    rows, channels = signal.shape
    chips = lax.axis_size("ctx") // 2
    block = 2 * rows
    mine = channels // (2 * chips)
    index = lax.axis_index("ctx")
    z, core = index // 2, lax.rem(index, 2)
    place = jnp.stack([z, core]).astype(jnp.int32)
    fwd_high, fwd_low = forward_tables(block)
    inv_high, _ = inverse_tables(block)

    tap_pieces = cut_for_chips(filter_taps, z, chips)
    taps = gather_tokens(tap_pieces, core, chips)

    values = after(signal, tap_pieces).astype(jnp.float32)
    row_power = sum_over(jnp.sum(values * values, axis=1), "ch") / C
    normed = (values * lax.rsqrt(row_power + EPS)[:, None] * norm_gain[None, :]).astype(
        jnp.bfloat16
    )
    whole = pltpu.VMEM((chips, block, mine), jnp.bfloat16)
    limits = pltpu.CompilerParams(vmem_limit_bytes=40 * 1024 * 1024)
    fil_spectra = pl.pallas_call(
        functools.partial(filter_kernel, chips),
        out_shape=jax.ShapeDtypeStruct((chips, 2 * block, mine), jnp.float32),
        in_specs=[SMEM] + [VMEM] * (2 + 2 * chips),
        out_specs=VMEM,
        scratch_shapes=[whole],
        compiler_params=limits,
        cost_estimate=cost(8 * block * block * mine * chips),
        name="filter_spectra",
    )(place, fwd_high, fwd_low, *taps)
    features = gather_tokens(
        cut_for_chips(normed, z, chips), core, chips, lambda _: fil_spectra
    )
    parts = pl.pallas_call(
        functools.partial(signal_kernel, chips),
        out_shape=[jax.ShapeDtypeStruct((block, mine), jnp.bfloat16)] * chips,
        in_specs=[SMEM] + [VMEM] * (4 + 2 * chips),
        out_specs=[VMEM] * chips,
        scratch_shapes=[
            whole,
            pltpu.VMEM((chips, 2 * block, mine), jnp.float32),
            pltpu.VMEM((chips, 2 * block, mine), jnp.bfloat16),
        ],
        compiler_params=limits,
        cost_estimate=cost(16 * block * block * mine * chips),
        name="convolve",
    )(place, fil_spectra, fwd_high, fwd_low, inv_high, *features)

    pieces = [parts[0]] + [None] * (chips - 1)
    for distance in distances(chips):
        pieces[distance] = along_chips(parts[distance], distance)
    arrived = []
    for piece in pieces:
        arrived.append(piece)
        arrived.append(other_core(lax.dynamic_slice_in_dim(piece, (1 - core) * rows, rows, 0)))
    if mine % 128 != 0:
        return mix_plain(chips, z, core, normed, out_gate, skip_gain[None, :], arrived)
    return pl.pallas_call(
        functools.partial(mix_kernel, chips),
        out_shape=jax.ShapeDtypeStruct((rows, channels), jnp.bfloat16),
        in_specs=[SMEM] + [VMEM] * (3 + 2 * chips),
        out_specs=VMEM,
        compiler_params=limits,
        cost_estimate=cost(4 * rows * channels),
        name="mix",
    )(place, normed, out_gate, skip_gain[None, :], *arrived)


def solution(mesh):
    return jax.shard_map(
        local,
        mesh=mesh,
        in_specs=(P("ctx", "ch"), P("ch"), P("ch"), P("ctx", "ch"), P("ctx", "ch")),
        out_specs=P("ctx", "ch"),
        check_vma=False,
    )
```

```python
import functools
import math

import jax
import jax.numpy as jnp
import numpy as np
from jax import lax
from jax.experimental import pallas as pl
from jax.experimental.pallas import tpu as pltpu
from jax.sharding import PartitionSpec as P

C = 8192

EPS = 1e-06

VMEM = pl.BlockSpec(memory_space=pltpu.VMEM)
SMEM = pl.BlockSpec(memory_space=pltpu.SMEM)
ANY = pl.BlockSpec(memory_space=pl.ANY)


def row_angles(block):
    order = np.concatenate([np.arange(0, block, 2), np.arange(1, block, 2)])
    tokens = np.arange(block)
    turns = (2 * order[:, None] + 1) * tokens[None, :] % (4 * block)
    return turns * (math.pi / (2 * block))


def two_parts(table):
    table = table.astype(np.float32)
    high = table.astype(jnp.bfloat16)
    low = (table - high.astype(np.float32)).astype(jnp.bfloat16)
    return jnp.asarray(high), jnp.asarray(low)


def forward_tables(block):
    angles = row_angles(block)
    return two_parts(np.concatenate([np.cos(angles), -np.sin(angles)]))


def inverse_tables(block):
    angles = row_angles(block).T
    return two_parts(np.concatenate([np.cos(angles), -np.sin(angles)], axis=1) / block)


def transform_blocks(place_ref, distances, pieces, tables, whole, spectra):
    z, core = place_ref[0], place_ref[1]
    rows = whole.shape[1] // 2
    own = pl.ds(pl.multiple_of(core * rows, rows), rows)
    other = pl.ds(pl.multiple_of((1 - core) * rows, rows), rows)
    for slot, (distance, (own_ref, other_ref)) in enumerate(zip(distances, pieces)):
        whole[slot, own, :] = own_ref[...]
        whole[slot, other, :] = other_ref[...]
        block = whole[slot]
        spectrum = jnp.dot(tables[0][...], block, preferred_element_type=jnp.float32)
        spectrum += jnp.dot(tables[1][...], block, preferred_element_type=jnp.float32)
        spectra[z ^ distance] = spectrum


def spectra_kernel(chips, place_ref, high_ref, low_ref, *rest):
    blocks, (*outs, whole, spectra) = rest[:chips], rest[chips:]
    rows, columns = whole.shape[1] // 2, outs[0].shape[2]
    tables = (high_ref, low_ref)
    transform_blocks(place_ref, range(chips), halves(blocks, rows), tables, whole, spectra)
    re_even, re_odd, im_even, im_odd = [pl.ds(i * rows, rows) for i in range(4)]
    for chunk, out_ref in enumerate(outs):
        cut = pl.ds(chunk * columns, columns)
        out_ref[0] = spectra[0, :, cut]
        for lag in range(1, chips):
            here, past = spectra.at[lag], spectra.at[lag - 1]
            out_ref[lag, re_even, :] = here[re_even, cut] - past[im_even, cut]
            out_ref[lag, im_even, :] = here[im_even, cut] + past[re_even, cut]
            out_ref[lag, re_odd, :] = here[re_odd, cut] + past[im_odd, cut]
            out_ref[lag, im_odd, :] = here[im_odd, cut] - past[re_odd, cut]


def halves(blocks, rows):
    return [(ref.at[pl.ds(0, rows), :], ref.at[pl.ds(rows, rows), :]) for ref in blocks]


def convolve_kernel(chips, place_ref, _, fil_ref, fwd_ref, inv_ref, *rest):
    blocks, outs = rest[:chips], rest[chips : 2 * chips]
    whole, spectra, products, results = rest[2 * chips :]
    z, core = place_ref[0], place_ref[1]
    packs, block, columns = whole.shape
    pack = chips // packs
    mine, rows = columns // pack, block // 2

    def lanes_of(chip):
        if pack == 1:
            return pl.ds(0, mine)
        side = chip % pack if isinstance(chip, int) else lax.rem(chip, pack)
        return pl.ds(side * mine if isinstance(chip, int) else pl.multiple_of(side * mine, mine), mine)

    own = pl.ds(pl.multiple_of(core * rows, rows), rows)
    other = pl.ds(pl.multiple_of((1 - core) * rows, rows), rows)
    for distance, ref in enumerate(blocks):
        source = z ^ distance
        whole[source // pack, own, lanes_of(source)] = ref[pl.ds(0, rows), :]
        whole[source // pack, other, lanes_of(source)] = ref[pl.ds(rows, rows), :]
    for group in range(packs):
        spectra[group] = jnp.dot(
            fwd_ref[...], whole[group], preferred_element_type=jnp.float32
        )
    tile, width = 16, min(mine, 128)

    @pl.loop(0, block // tile)
    def _(step):
        start = pl.multiple_of(step * tile, tile)
        re_rows, im_rows = pl.ds(start, tile), pl.ds(block + start, tile)
        for first in range(0, mine, width):
            cut = pl.ds(first, width)
            sig = []
            for source in range(chips):
                lanes = pl.ds((source % pack) * mine + first, width)
                sig.append((spectra[source // pack, re_rows, lanes], spectra[source // pack, im_rows, lanes]))
            for target in range(chips):
                sum_re = sum_im = None
                for source in range(target + 1):
                    sig_re, sig_im = sig[source]
                    fil_re = fil_ref[target - source, re_rows, cut]
                    fil_im = fil_ref[target - source, im_rows, cut]
                    re = sig_re * fil_re - sig_im * fil_im
                    im = sig_re * fil_im + sig_im * fil_re
                    sum_re = re if sum_re is None else sum_re + re
                    sum_im = im if sum_im is None else sum_im + im
                lanes = pl.ds((target % pack) * mine + first, width)
                products[target // pack, re_rows, lanes] = sum_re.astype(jnp.bfloat16)
                products[target // pack, im_rows, lanes] = sum_im.astype(jnp.bfloat16)

    for group in range(packs):
        result = jnp.dot(inv_ref[...], products[group], preferred_element_type=jnp.float32)
        results[group] = result.astype(jnp.bfloat16)
    for distance, out_ref in enumerate(outs):
        target = z ^ distance
        out_ref[...] = results[target // pack, :, lanes_of(target)]


def mix_kernel(chips, chunks, place_ref, normed_ref, gate_ref, skip_ref, *rest):
    out_ref, staged, sems = rest[-3:]
    z, core = place_ref[0], place_ref[1]
    _, rows, mine = staged.shape
    copies = []
    for chunk in range(chunks):
        other_ref, *pieces = rest[chunk * (chips + 1) : (chunk + 1) * (chips + 1)]
        for distance, piece_ref in enumerate(pieces):
            own = piece_ref[pl.ds(pl.multiple_of(core * rows, rows), rows), :]
            other = other_ref[pl.ds(distance * rows, rows), :]
            for owner, conv in ((core, own), (1 - core, other)):
                column = ((owner * chunks + chunk) * chips + (z ^ distance)) * mine
                cut = pl.ds(pl.multiple_of(column, mine), mine)
                direct = skip_ref[:, cut] * normed_ref[:, cut].astype(jnp.float32)
                mixed = gate_ref[:, cut].astype(jnp.float32) * (conv.astype(jnp.float32) + direct)
                slot = len(copies)
                staged[slot] = mixed.astype(jnp.bfloat16)
                copies.append(
                    pltpu.make_async_copy(staged.at[slot], out_ref.at[:, cut], sems.at[slot])
                )
                copies[-1].start()
    for copy in copies:
        copy.wait()


def mix_plain(chips, chunks, z, core, normed, gate, skip, arrived):
    rows, channels = normed.shape
    mine = channels // (2 * chips * chunks)
    convolved = jnp.zeros((rows, channels), jnp.bfloat16)
    for chunk in range(chunks):
        others, *pieces = arrived[chunk * (chips + 1) : (chunk + 1) * (chips + 1)]
        for distance, piece in enumerate(pieces):
            own = lax.dynamic_slice_in_dim(piece, core * rows, rows, 0)
            other = others[distance * rows : (distance + 1) * rows]
            for owner, conv in ((core, own), (1 - core, other)):
                first = ((owner * chunks + chunk) * chips + (z ^ distance)) * mine
                convolved = lax.dynamic_update_slice_in_dim(convolved, conv, first, 1)
    direct = skip * normed.astype(jnp.float32)
    return (gate.astype(jnp.float32) * (convolved.astype(jnp.float32) + direct)).astype(
        jnp.bfloat16
    )


def along_chips(piece, distance):
    route = [(i, i ^ (2 * distance)) for i in range(lax.axis_size("ctx"))]
    return lax.ppermute(piece, "ctx", route)


def other_core(piece):
    return lax.ppermute(piece, "ctx", [(i, i ^ 1) for i in range(lax.axis_size("ctx"))])


def tie(*values):
    return lax.optimization_barrier(values)


def tie(*values):
    return lax.optimization_barrier(values)


def kernel_cost():
    return pl.CostEstimate(flops=1000, bytes_accessed=1024, transcendentals=0)


def local(signal, norm_gain, skip_gain, filter_taps, out_gate):
    rows, channels = signal.shape
    chips = lax.axis_size("ctx") // 2
    groups = lax.axis_size("ch")
    chunks = 2
    block = 2 * rows
    half = channels // 2
    part = half // chunks
    mine = part // chips
    pack = 2 if mine % 128 == 0 else 1
    if chips & (chips - 1) or groups & (groups - 1):
        raise ValueError("power of 2")
    index = lax.axis_index("ctx")
    z, core = index // 2, lax.rem(index, 2)
    place = jnp.stack([z, core]).astype(jnp.int32)
    fwd_high, fwd_low = forward_tables(block)
    inv_high, _ = inverse_tables(block)
    limits = pltpu.CompilerParams(vmem_limit_bytes=40 * 1024 * 1024)
    far = list(range(chips - 1, chips // 2 - 1, -1))
    order = far[:1] + list(range(1, chips // 2)) + far[1:]
    cut = functools.partial(lax.dynamic_slice_in_dim, axis=1)

    own_taps = cut(filter_taps, core * half, half)
    other_taps = other_core(cut(filter_taps, (1 - core) * half, half))
    both_taps = jnp.concatenate([own_taps, other_taps])
    taps = [
        jnp.concatenate(
            [cut(both_taps, chunk * part + (z ^ d) * mine, mine) for chunk in range(chunks)], axis=1
        )
        for d in range(chips)
    ]
    row_power = jnp.sum(jnp.square(signal.astype(jnp.float32)), axis=1)
    values, row_power, taps[order[0]] = tie(signal, row_power, taps[order[0]])

    row_power = jnp.concatenate([row_power, other_core(row_power)])
    own_half = cut(values, core * half, half)
    other_half = other_core(cut(values, (1 - core) * half, half))
    step = 1
    while step < groups:
        route = [(i, i ^ step) for i in range(groups)]
        row_power = row_power + lax.ppermute(row_power, "ch", route)
        if step == 1:
            row_power, other_half = tie(row_power, other_half)
        step *= 2
    for d in order:
        taps[d] = along_chips(taps[d], d)
    scale = lax.rsqrt(row_power / C + EPS)
    normed = (signal.astype(jnp.float32) * scale[:rows, None] * norm_gain[None, :]).astype(
        jnp.bfloat16
    )
    both = jnp.concatenate([own_half, other_half])
    for d in order[:-1]:
        both, taps[d] = tie(both, taps[d])
    half_gain = lax.dynamic_slice_in_dim(norm_gain, core * half, half, 0)
    both = (both.astype(jnp.float32) * scale[:, None] * half_gain[None, :]).astype(jnp.bfloat16)
    blocks = []
    for chunk in range(chunks):
        pieces = [cut(both, chunk * part + (z ^ d) * mine, mine) for d in range(chips)]
        for d in order:
            pieces[d] = along_chips(pieces[d], d)
        blocks.append(pieces)

    fil_spectra = pl.pallas_call(
        functools.partial(spectra_kernel, chips),
        out_shape=[jax.ShapeDtypeStruct((chips, 2 * block, mine), jnp.float32)] * chunks,
        in_specs=[SMEM] + [VMEM] * (2 + chips),
        out_specs=[VMEM] * chunks,
        scratch_shapes=[
            pltpu.VMEM((chips, block, chunks * mine), jnp.bfloat16),
            pltpu.VMEM((chips, 2 * block, chunks * mine), jnp.float32),
        ],
        compiler_params=limits,
        cost_estimate=kernel_cost(),
        name="spectra",
    )(place, fwd_high, fwd_low, *taps)
    *fil_spectra, = tie(*fil_spectra, *blocks[0])
    fil_spectra, blocks[0] = fil_spectra[:chunks], fil_spectra[chunks:]

    results, earlier = [], place
    for chunk in range(chunks):
        pieces = pl.pallas_call(
            functools.partial(convolve_kernel, chips),
            out_shape=[jax.ShapeDtypeStruct((block, mine), jnp.bfloat16)] * chips,
            in_specs=[SMEM, ANY] + [VMEM] * (3 + chips),
            out_specs=[VMEM] * chips,
            scratch_shapes=[
                pltpu.VMEM((chips // pack, block, pack * mine), jnp.bfloat16),
                pltpu.VMEM((chips // pack, 2 * block, pack * mine), jnp.float32),
                pltpu.VMEM((chips // pack, 2 * block, pack * mine), jnp.bfloat16),
                pltpu.VMEM((chips // pack, block, pack * mine), jnp.bfloat16),
            ],
            compiler_params=limits,
            cost_estimate=kernel_cost(),
            name="convolve",
        )(place, earlier, fil_spectra[chunk], fwd_high, inv_high, *blocks[chunk])
        earlier = pieces[0]
        results.append(list(pieces))

    arrived = []
    for chunk, pieces in enumerate(results):
        for d in order:
            pieces[d] = along_chips(pieces[d], d)
        if chunk + 1 < chunks:
            *pieces, results[chunk + 1][0] = tie(*pieces, results[chunk + 1][0])
        if chunk:
            arrived[0], pieces[order[-1]] = tie(arrived[0], pieces[order[-1]])
        cuts = [lax.dynamic_slice_in_dim(piece, (1 - core) * rows, rows, 0) for piece in pieces]
        arrived += [other_core(jnp.concatenate(cuts)), *pieces]
    skip = skip_gain[None, :]
    if mine % 128 != 0:
        return mix_plain(chips, chunks, z, core, normed, out_gate, skip, arrived)
    return pl.pallas_call(
        functools.partial(mix_kernel, chips, chunks),
        out_shape=jax.ShapeDtypeStruct((rows, channels), jnp.bfloat16),
        in_specs=[SMEM] + [VMEM] * (3 + len(arrived)),
        out_specs=ANY,
        scratch_shapes=[
            pltpu.VMEM((2 * chips * chunks, rows, mine), jnp.bfloat16),
            pltpu.SemaphoreType.DMA((2 * chips * chunks,)),
        ],
        compiler_params=limits,
        cost_estimate=kernel_cost(),
        name="mix",
    )(place, normed, out_gate, skip, *arrived)


def solution(mesh):
    return jax.shard_map(
        local,
        mesh=mesh,
        in_specs=(P("ctx", "ch"), P("ch"), P("ch"), P("ctx", "ch"), P("ctx", "ch")),
        out_specs=P("ctx", "ch"),
        check_vma=False,
    )
```

```python
import functools
import math

import jax
import jax.numpy as jnp
import numpy as np
from jax import lax
from jax.experimental import pallas as pl
from jax.experimental.pallas import tpu as pltpu
from jax.sharding import PartitionSpec as P

C = 8192

EPS = 1e-06

VMEM = pl.BlockSpec(memory_space=pltpu.VMEM)
SMEM = pl.BlockSpec(memory_space=pltpu.SMEM)
ANY = pl.BlockSpec(memory_space=pl.ANY)


def row_angles(block):
    order = np.concatenate([np.arange(0, block, 2), np.arange(1, block, 2)])
    tokens = np.arange(block)
    turns = (2 * order[:, None] + 1) * tokens[None, :] % (4 * block)
    return turns * (math.pi / (2 * block))


def two_parts(table):
    table = table.astype(np.float32)
    high = table.astype(jnp.bfloat16)
    low = (table - high.astype(np.float32)).astype(jnp.bfloat16)
    return jnp.asarray(high), jnp.asarray(low)


def forward_tables(block):
    angles = row_angles(block)
    return two_parts(np.concatenate([np.cos(angles), -np.sin(angles)]))


def inverse_tables(block):
    angles = row_angles(block).T
    return two_parts(np.concatenate([np.cos(angles), -np.sin(angles)], axis=1) / block)


def transform_blocks(place_ref, distances, pieces, tables, whole, spectra):
    z, core = place_ref[0], place_ref[1]
    rows = whole.shape[1] // 2
    own = pl.ds(pl.multiple_of(core * rows, rows), rows)
    other = pl.ds(pl.multiple_of((1 - core) * rows, rows), rows)
    for slot, (distance, (own_ref, other_ref)) in enumerate(zip(distances, pieces)):
        whole[slot, own, :] = own_ref[...]
        whole[slot, other, :] = other_ref[...]
        block = whole[slot]
        spectrum = jnp.dot(tables[0][...], block, preferred_element_type=jnp.float32)
        spectrum += jnp.dot(tables[1][...], block, preferred_element_type=jnp.float32)
        spectra[z ^ distance] = spectrum


def spectra_kernel(chips, place_ref, high_ref, low_ref, *rest):
    blocks, (*outs, whole, spectra) = rest[:chips], rest[chips:]
    rows, columns = whole.shape[1] // 2, outs[0].shape[2]
    tables = (high_ref, low_ref)
    transform_blocks(place_ref, range(chips), halves(blocks, rows), tables, whole, spectra)
    re_even, re_odd, im_even, im_odd = [pl.ds(i * rows, rows) for i in range(4)]
    for chunk, out_ref in enumerate(outs):
        cut = pl.ds(chunk * columns, columns)
        out_ref[0] = spectra[0, :, cut]
        for lag in range(1, chips):
            here, past = spectra.at[lag], spectra.at[lag - 1]
            out_ref[lag, re_even, :] = here[re_even, cut] - past[im_even, cut]
            out_ref[lag, im_even, :] = here[im_even, cut] + past[re_even, cut]
            out_ref[lag, re_odd, :] = here[re_odd, cut] + past[im_odd, cut]
            out_ref[lag, im_odd, :] = here[im_odd, cut] - past[re_odd, cut]


def halves(blocks, rows):
    return [(ref.at[pl.ds(0, rows), :], ref.at[pl.ds(rows, rows), :]) for ref in blocks]


def convolve_kernel(chips, place_ref, _, fil_ref, fwd_ref, inv_ref, *rest):
    blocks, outs = rest[:chips], rest[chips : 2 * chips]
    whole, spectra, products, results = rest[2 * chips :]
    z, core = place_ref[0], place_ref[1]
    packs, block, columns = whole.shape
    pack = chips // packs
    mine, rows = columns // pack, block // 2

    def lanes_of(chip):
        if pack == 1:
            return pl.ds(0, mine)
        side = chip % pack if isinstance(chip, int) else lax.rem(chip, pack)
        return pl.ds(side * mine if isinstance(chip, int) else pl.multiple_of(side * mine, mine), mine)

    own = pl.ds(pl.multiple_of(core * rows, rows), rows)
    other = pl.ds(pl.multiple_of((1 - core) * rows, rows), rows)
    for distance, ref in enumerate(blocks):
        source = z ^ distance
        whole[source // pack, own, lanes_of(source)] = ref[pl.ds(0, rows), :]
        whole[source // pack, other, lanes_of(source)] = ref[pl.ds(rows, rows), :]
    for group in range(packs):
        spectra[group] = jnp.dot(
            fwd_ref[...], whole[group], preferred_element_type=jnp.float32
        )
    tile, width = 16, min(mine, 128)

    @pl.loop(0, block // tile)
    def _(step):
        start = pl.multiple_of(step * tile, tile)
        re_rows, im_rows = pl.ds(start, tile), pl.ds(block + start, tile)
        for first in range(0, mine, width):
            cut = pl.ds(first, width)
            sig = []
            for source in range(chips):
                lanes = pl.ds((source % pack) * mine + first, width)
                sig.append((spectra[source // pack, re_rows, lanes], spectra[source // pack, im_rows, lanes]))
            for target in range(chips):
                sum_re = sum_im = None
                for source in range(target + 1):
                    sig_re, sig_im = sig[source]
                    fil_re = fil_ref[target - source, re_rows, cut]
                    fil_im = fil_ref[target - source, im_rows, cut]
                    re = sig_re * fil_re - sig_im * fil_im
                    im = sig_re * fil_im + sig_im * fil_re
                    sum_re = re if sum_re is None else sum_re + re
                    sum_im = im if sum_im is None else sum_im + im
                lanes = pl.ds((target % pack) * mine + first, width)
                products[target // pack, re_rows, lanes] = sum_re.astype(jnp.bfloat16)
                products[target // pack, im_rows, lanes] = sum_im.astype(jnp.bfloat16)

    for group in range(packs):
        result = jnp.dot(inv_ref[...], products[group], preferred_element_type=jnp.float32)
        results[group] = result.astype(jnp.bfloat16)
    for distance, out_ref in enumerate(outs):
        target = z ^ distance
        out_ref[...] = results[target // pack, :, lanes_of(target)]


def mix_kernel(chips, chunks, place_ref, normed_ref, gate_ref, skip_ref, *rest):
    out_ref, staged, sems = rest[-3:]
    z, core = place_ref[0], place_ref[1]
    _, rows, mine = staged.shape
    copies = []
    for chunk in range(chunks):
        other_ref, *pieces = rest[chunk * (chips + 1) : (chunk + 1) * (chips + 1)]
        for distance, piece_ref in enumerate(pieces):
            own = piece_ref[pl.ds(pl.multiple_of(core * rows, rows), rows), :]
            other = other_ref[pl.ds(distance * rows, rows), :]
            for owner, conv in ((core, own), (1 - core, other)):
                column = ((owner * chunks + chunk) * chips + (z ^ distance)) * mine
                cut = pl.ds(pl.multiple_of(column, mine), mine)
                direct = skip_ref[:, cut] * normed_ref[:, cut].astype(jnp.float32)
                mixed = gate_ref[:, cut].astype(jnp.float32) * (conv.astype(jnp.float32) + direct)
                slot = len(copies)
                staged[slot] = mixed.astype(jnp.bfloat16)
                copies.append(
                    pltpu.make_async_copy(staged.at[slot], out_ref.at[:, cut], sems.at[slot])
                )
                copies[-1].start()
    for copy in copies:
        copy.wait()


def mix_plain(chips, chunks, z, core, normed, gate, skip, arrived):
    rows, channels = normed.shape
    mine = channels // (2 * chips * chunks)
    convolved = jnp.zeros((rows, channels), jnp.bfloat16)
    for chunk in range(chunks):
        others, *pieces = arrived[chunk * (chips + 1) : (chunk + 1) * (chips + 1)]
        for distance, piece in enumerate(pieces):
            own = lax.dynamic_slice_in_dim(piece, core * rows, rows, 0)
            other = others[distance * rows : (distance + 1) * rows]
            for owner, conv in ((core, own), (1 - core, other)):
                first = ((owner * chunks + chunk) * chips + (z ^ distance)) * mine
                convolved = lax.dynamic_update_slice_in_dim(convolved, conv, first, 1)
    direct = skip * normed.astype(jnp.float32)
    return (gate.astype(jnp.float32) * (convolved.astype(jnp.float32) + direct)).astype(
        jnp.bfloat16
    )


def along_chips(piece, distance):
    route = [(i, i ^ (2 * distance)) for i in range(lax.axis_size("ctx"))]
    return lax.ppermute(piece, "ctx", route)


def other_core(piece):
    return lax.ppermute(piece, "ctx", [(i, i ^ 1) for i in range(lax.axis_size("ctx"))])


def tie(*values):
    return lax.optimization_barrier(values)


def tie(*values):
    return lax.optimization_barrier(values)


def kernel_cost():
    return pl.CostEstimate(flops=1000, bytes_accessed=1024, transcendentals=0)


def local(signal, norm_gain, skip_gain, filter_taps, out_gate):
    rows, channels = signal.shape
    chips = lax.axis_size("ctx") // 2
    groups = lax.axis_size("ch")
    chunks = 2
    block = 2 * rows
    half = channels // 2
    part = half // chunks
    mine = part // chips
    pack = 2 if mine % 128 == 0 else 1
    if chips & (chips - 1) or groups & (groups - 1):
        raise ValueError("power of 2")
    index = lax.axis_index("ctx")
    z, core = index // 2, lax.rem(index, 2)
    place = jnp.stack([z, core]).astype(jnp.int32)
    fwd_high, fwd_low = forward_tables(block)
    inv_high, _ = inverse_tables(block)
    limits = pltpu.CompilerParams(vmem_limit_bytes=40 * 1024 * 1024)
    far = list(range(chips - 1, chips // 2 - 1, -1))
    order = far[:1] + list(range(1, chips // 2)) + far[1:]
    cut = functools.partial(lax.dynamic_slice_in_dim, axis=1)

    first = order[0]
    first_cut = jnp.concatenate(
        [
            cut(filter_taps, owner * half + chunk * part + (z ^ first) * mine, mine)
            for owner in range(2)
            for chunk in range(chunks)
        ],
        axis=1,
    )
    later_taps, first_cut = tie(filter_taps, first_cut)
    own_taps = cut(later_taps, core * half, half)
    other_taps = other_core(cut(later_taps, (1 - core) * half, half))
    both_taps = jnp.concatenate([own_taps, other_taps])
    taps = [
        jnp.concatenate(
            [cut(both_taps, chunk * part + (z ^ d) * mine, mine) for chunk in range(chunks)], axis=1
        )
        for d in range(chips)
    ]
    row_power = jnp.sum(jnp.square(signal.astype(jnp.float32)), axis=1)
    taps[first] = first_cut
    values, row_power, taps[order[1]] = tie(signal, row_power, taps[order[1]])

    row_power = jnp.concatenate([row_power, other_core(row_power)])
    row_power, taps[order[-1]] = tie(row_power, taps[order[-1]])
    own_half = cut(values, core * half, half)
    other_half = other_core(cut(values, (1 - core) * half, half))
    step = 1
    while step < groups:
        route = [(i, i ^ step) for i in range(groups)]
        row_power = row_power + lax.ppermute(row_power, "ch", route)
        if step == 1:
            row_power, other_half = tie(row_power, other_half)
        step *= 2
    for d in order:
        taps[d] = along_chips(taps[d], d)
    scale = lax.rsqrt(row_power / C + EPS)
    normed = (signal.astype(jnp.float32) * scale[:rows, None] * norm_gain[None, :]).astype(
        jnp.bfloat16
    )
    both = jnp.concatenate([own_half, other_half])
    for d in order[:1]:
        both, taps[d] = tie(both, taps[d])
    half_gain = lax.dynamic_slice_in_dim(norm_gain, core * half, half, 0)
    both = (both.astype(jnp.float32) * scale[:, None] * half_gain[None, :]).astype(jnp.bfloat16)
    blocks = []
    for chunk in range(chunks):
        pieces = [cut(both, chunk * part + (z ^ d) * mine, mine) for d in range(chips)]
        for d in order:
            pieces[d] = along_chips(pieces[d], d)
        blocks.append(pieces)

    width = chunks * mine
    mixed_cores = taps[first]
    swapped = cut(mixed_cores, (1 - core) * width, width)
    taps[first] = jnp.concatenate([cut(mixed_cores, core * width, width), other_core(swapped)])
    fil_spectra = pl.pallas_call(
        functools.partial(spectra_kernel, chips),
        out_shape=[jax.ShapeDtypeStruct((chips, 2 * block, mine), jnp.float32)] * chunks,
        in_specs=[SMEM] + [VMEM] * (2 + chips),
        out_specs=[VMEM] * chunks,
        scratch_shapes=[
            pltpu.VMEM((chips, block, chunks * mine), jnp.bfloat16),
            pltpu.VMEM((chips, 2 * block, chunks * mine), jnp.float32),
        ],
        compiler_params=limits,
        cost_estimate=kernel_cost(),
        name="spectra",
    )(place, fwd_high, fwd_low, *taps)
    *fil_spectra, = tie(*fil_spectra, *blocks[0])
    fil_spectra, blocks[0] = fil_spectra[:chunks], fil_spectra[chunks:]

    results, earlier = [], place
    for chunk in range(chunks):
        pieces = pl.pallas_call(
            functools.partial(convolve_kernel, chips),
            out_shape=[jax.ShapeDtypeStruct((block, mine), jnp.bfloat16)] * chips,
            in_specs=[SMEM, ANY] + [VMEM] * (3 + chips),
            out_specs=[VMEM] * chips,
            scratch_shapes=[
                pltpu.VMEM((chips // pack, block, pack * mine), jnp.bfloat16),
                pltpu.VMEM((chips // pack, 2 * block, pack * mine), jnp.float32),
                pltpu.VMEM((chips // pack, 2 * block, pack * mine), jnp.bfloat16),
                pltpu.VMEM((chips // pack, block, pack * mine), jnp.bfloat16),
            ],
            compiler_params=limits,
            cost_estimate=kernel_cost(),
            name="convolve",
        )(place, earlier, fil_spectra[chunk], fwd_high, inv_high, *blocks[chunk])
        earlier = pieces[0]
        results.append(list(pieces))

    arrived = []
    for chunk, pieces in enumerate(results):
        for d in order:
            pieces[d] = along_chips(pieces[d], d)
        if chunk + 1 < chunks:
            *pieces, results[chunk + 1][0] = tie(*pieces, results[chunk + 1][0])
        if chunk:
            arrived[0], pieces[order[-1]] = tie(arrived[0], pieces[order[-1]])
        cuts = [lax.dynamic_slice_in_dim(piece, (1 - core) * rows, rows, 0) for piece in pieces]
        arrived += [other_core(jnp.concatenate(cuts)), *pieces]
    skip = skip_gain[None, :]
    if mine % 128 != 0:
        return mix_plain(chips, chunks, z, core, normed, out_gate, skip, arrived)
    return pl.pallas_call(
        functools.partial(mix_kernel, chips, chunks),
        out_shape=jax.ShapeDtypeStruct((rows, channels), jnp.bfloat16),
        in_specs=[SMEM] + [VMEM] * (3 + len(arrived)),
        out_specs=ANY,
        scratch_shapes=[
            pltpu.VMEM((2 * chips * chunks, rows, mine), jnp.bfloat16),
            pltpu.SemaphoreType.DMA((2 * chips * chunks,)),
        ],
        compiler_params=limits,
        cost_estimate=kernel_cost(),
        name="mix",
    )(place, normed, out_gate, skip, *arrived)


def solution(mesh):
    return jax.shard_map(
        local,
        mesh=mesh,
        in_specs=(P("ctx", "ch"), P("ch"), P("ch"), P("ctx", "ch"), P("ctx", "ch")),
        out_specs=P("ctx", "ch"),
        check_vma=False,
    )
```

```python
import functools
import math

import jax
import jax.numpy as jnp
import numpy as np
from jax import lax
from jax.experimental import pallas as pl
from jax.experimental.pallas import tpu as pltpu
from jax.sharding import PartitionSpec as P

C = 8192

EPS = 1e-06

VMEM = pl.BlockSpec(memory_space=pltpu.VMEM)
SMEM = pl.BlockSpec(memory_space=pltpu.SMEM)
ANY = pl.BlockSpec(memory_space=pl.ANY)


def row_angles(block):
    order = np.concatenate([np.arange(0, block, 2), np.arange(1, block, 2)])
    tokens = np.arange(block)
    turns = (2 * order[:, None] + 1) * tokens[None, :] % (4 * block)
    return turns * (math.pi / (2 * block))


def two_parts(table):
    table = table.astype(np.float32)
    high = table.astype(jnp.bfloat16)
    low = (table - high.astype(np.float32)).astype(jnp.bfloat16)
    return jnp.asarray(high), jnp.asarray(low)


def forward_tables(block):
    angles = row_angles(block)
    return two_parts(np.concatenate([np.cos(angles), -np.sin(angles)]))


def inverse_tables(block):
    angles = row_angles(block).T
    return two_parts(np.concatenate([np.cos(angles), -np.sin(angles)], axis=1) / block)


def transform_blocks(place_ref, distances, pieces, tables, whole, spectra):
    z, core = place_ref[0], place_ref[1]
    rows = whole.shape[1] // 2
    own = pl.ds(pl.multiple_of(core * rows, rows), rows)
    other = pl.ds(pl.multiple_of((1 - core) * rows, rows), rows)
    for slot, (distance, (own_ref, other_ref)) in enumerate(zip(distances, pieces)):
        whole[slot, own, :] = own_ref[...]
        whole[slot, other, :] = other_ref[...]
        block = whole[slot]
        spectrum = jnp.dot(tables[0][...], block, preferred_element_type=jnp.float32)
        spectrum += jnp.dot(tables[1][...], block, preferred_element_type=jnp.float32)
        spectra[z ^ distance] = spectrum


def spectra_kernel(chips, place_ref, high_ref, low_ref, *rest):
    blocks, (*outs, whole, spectra) = rest[:chips], rest[chips:]
    rows, columns = whole.shape[1] // 2, outs[0].shape[2]
    tables = (high_ref, low_ref)
    transform_blocks(place_ref, range(chips), halves(blocks, rows), tables, whole, spectra)
    re_even, re_odd, im_even, im_odd = [pl.ds(i * rows, rows) for i in range(4)]
    for chunk, out_ref in enumerate(outs):
        cut = pl.ds(chunk * columns, columns)
        out_ref[0] = spectra[0, :, cut]
        for lag in range(1, chips):
            here, past = spectra.at[lag], spectra.at[lag - 1]
            out_ref[lag, re_even, :] = here[re_even, cut] - past[im_even, cut]
            out_ref[lag, im_even, :] = here[im_even, cut] + past[re_even, cut]
            out_ref[lag, re_odd, :] = here[re_odd, cut] + past[im_odd, cut]
            out_ref[lag, im_odd, :] = here[im_odd, cut] - past[re_odd, cut]


def halves(blocks, rows):
    return [(ref.at[pl.ds(0, rows), :], ref.at[pl.ds(rows, rows), :]) for ref in blocks]


def convolve_kernel(chips, place_ref, _, fil_ref, fwd_ref, low_ref, inv_ref, *rest):
    blocks, outs = rest[:chips], rest[chips : 2 * chips]
    whole, spectra, products, results = rest[2 * chips :]
    z, core = place_ref[0], place_ref[1]
    packs, block, columns = whole.shape
    pack = chips // packs
    mine, rows = columns // pack, block // 2

    def lanes_of(chip):
        if pack == 1:
            return pl.ds(0, mine)
        side = chip % pack if isinstance(chip, int) else lax.rem(chip, pack)
        return pl.ds(side * mine if isinstance(chip, int) else pl.multiple_of(side * mine, mine), mine)

    own = pl.ds(pl.multiple_of(core * rows, rows), rows)
    other = pl.ds(pl.multiple_of((1 - core) * rows, rows), rows)
    for distance, ref in enumerate(blocks):
        source = z ^ distance
        whole[source // pack, own, lanes_of(source)] = ref[pl.ds(0, rows), :]
        whole[source // pack, other, lanes_of(source)] = ref[pl.ds(rows, rows), :]
    for group in range(packs):
        spectra[group] = jnp.dot(
            fwd_ref[...], whole[group], preferred_element_type=jnp.float32
        ) + jnp.dot(low_ref[...], whole[group], preferred_element_type=jnp.float32)
    tile, width = 16, min(mine, 128)

    @pl.loop(0, block // tile)
    def _(step):
        start = pl.multiple_of(step * tile, tile)
        re_rows, im_rows = pl.ds(start, tile), pl.ds(block + start, tile)
        for first in range(0, mine, width):
            cut = pl.ds(first, width)
            sig = []
            for source in range(chips):
                lanes = pl.ds((source % pack) * mine + first, width)
                sig.append((spectra[source // pack, re_rows, lanes], spectra[source // pack, im_rows, lanes]))
            for target in range(chips):
                sum_re = sum_im = None
                for source in range(target + 1):
                    sig_re, sig_im = sig[source]
                    fil_re = fil_ref[target - source, re_rows, cut]
                    fil_im = fil_ref[target - source, im_rows, cut]
                    re = sig_re * fil_re - sig_im * fil_im
                    im = sig_re * fil_im + sig_im * fil_re
                    sum_re = re if sum_re is None else sum_re + re
                    sum_im = im if sum_im is None else sum_im + im
                lanes = pl.ds((target % pack) * mine + first, width)
                products[target // pack, re_rows, lanes] = sum_re.astype(jnp.bfloat16)
                products[target // pack, im_rows, lanes] = sum_im.astype(jnp.bfloat16)

    for group in range(packs):
        result = jnp.dot(inv_ref[...], products[group], preferred_element_type=jnp.float32)
        results[group] = result.astype(jnp.bfloat16)
    for distance, out_ref in enumerate(outs):
        target = z ^ distance
        out_ref[...] = results[target // pack, :, lanes_of(target)]


def mix_kernel(chips, chunks, place_ref, normed_ref, gate_ref, skip_ref, *rest):
    out_ref, staged, sems = rest[-3:]
    z, core = place_ref[0], place_ref[1]
    _, rows, mine = staged.shape
    copies = []
    for chunk in range(chunks):
        other_ref, *pieces = rest[chunk * (chips + 1) : (chunk + 1) * (chips + 1)]
        for distance, piece_ref in enumerate(pieces):
            own = piece_ref[pl.ds(pl.multiple_of(core * rows, rows), rows), :]
            other = other_ref[pl.ds(distance * rows, rows), :]
            for owner, conv in ((core, own), (1 - core, other)):
                column = ((owner * chunks + chunk) * chips + (z ^ distance)) * mine
                cut = pl.ds(pl.multiple_of(column, mine), mine)
                direct = skip_ref[:, cut] * normed_ref[:, cut].astype(jnp.float32)
                mixed = gate_ref[:, cut].astype(jnp.float32) * (conv.astype(jnp.float32) + direct)
                slot = len(copies)
                staged[slot] = mixed.astype(jnp.bfloat16)
                copies.append(
                    pltpu.make_async_copy(staged.at[slot], out_ref.at[:, cut], sems.at[slot])
                )
                copies[-1].start()
    for copy in copies:
        copy.wait()


def mix_plain(chips, chunks, z, core, normed, gate, skip, arrived):
    rows, channels = normed.shape
    mine = channels // (2 * chips * chunks)
    convolved = jnp.zeros((rows, channels), jnp.bfloat16)
    for chunk in range(chunks):
        others, *pieces = arrived[chunk * (chips + 1) : (chunk + 1) * (chips + 1)]
        for distance, piece in enumerate(pieces):
            own = lax.dynamic_slice_in_dim(piece, core * rows, rows, 0)
            other = others[distance * rows : (distance + 1) * rows]
            for owner, conv in ((core, own), (1 - core, other)):
                first = ((owner * chunks + chunk) * chips + (z ^ distance)) * mine
                convolved = lax.dynamic_update_slice_in_dim(convolved, conv, first, 1)
    direct = skip * normed.astype(jnp.float32)
    return (gate.astype(jnp.float32) * (convolved.astype(jnp.float32) + direct)).astype(
        jnp.bfloat16
    )


def along_chips(piece, distance):
    route = [(i, i ^ (2 * distance)) for i in range(lax.axis_size("ctx"))]
    return lax.ppermute(piece, "ctx", route)


def other_core(piece):
    return lax.ppermute(piece, "ctx", [(i, i ^ 1) for i in range(lax.axis_size("ctx"))])


def tie(*values):
    return lax.optimization_barrier(values)


def tie(*values):
    return lax.optimization_barrier(values)


def kernel_cost():
    return pl.CostEstimate(flops=1000, bytes_accessed=1024, transcendentals=0)


def local(signal, norm_gain, skip_gain, filter_taps, out_gate):
    rows, channels = signal.shape
    chips = lax.axis_size("ctx") // 2
    groups = lax.axis_size("ch")
    chunks = 2
    block = 2 * rows
    half = channels // 2
    part = half // chunks
    mine = part // chips
    pack = 2 if mine % 128 == 0 else 1
    if chips & (chips - 1) or groups & (groups - 1):
        raise ValueError("power of 2")
    index = lax.axis_index("ctx")
    z, core = index // 2, lax.rem(index, 2)
    place = jnp.stack([z, core]).astype(jnp.int32)
    fwd_high, fwd_low = forward_tables(block)
    inv_high, _ = inverse_tables(block)
    limits = pltpu.CompilerParams(vmem_limit_bytes=40 * 1024 * 1024)
    far = list(range(chips - 1, chips // 2 - 1, -1))
    order = far[:1] + list(range(1, chips // 2)) + far[1:]
    cut = functools.partial(lax.dynamic_slice_in_dim, axis=1)

    first = order[0]
    first_cut = jnp.concatenate(
        [
            cut(filter_taps, owner * half + chunk * part + (z ^ first) * mine, mine)
            for owner in range(2)
            for chunk in range(chunks)
        ],
        axis=1,
    )
    later_taps, first_cut = tie(filter_taps, first_cut)
    own_taps = cut(later_taps, core * half, half)
    other_taps = other_core(cut(later_taps, (1 - core) * half, half))
    both_taps = jnp.concatenate([own_taps, other_taps])
    taps = [
        jnp.concatenate(
            [cut(both_taps, chunk * part + (z ^ d) * mine, mine) for chunk in range(chunks)], axis=1
        )
        for d in range(chips)
    ]
    row_power = jnp.sum(jnp.square(signal.astype(jnp.float32)), axis=1)
    taps[first] = first_cut
    values, row_power, taps[order[1]] = tie(signal, row_power, taps[order[1]])

    row_power = jnp.concatenate([row_power, other_core(row_power)])
    row_power, taps[order[-1]] = tie(row_power, taps[order[-1]])
    own_half = cut(values, core * half, half)
    other_half = other_core(cut(values, (1 - core) * half, half))
    step = 1
    while step < groups:
        route = [(i, i ^ step) for i in range(groups)]
        row_power = row_power + lax.ppermute(row_power, "ch", route)
        if step == 1:
            row_power, other_half = tie(row_power, other_half)
        step *= 2
    for d in order:
        taps[d] = along_chips(taps[d], d)
    scale = lax.rsqrt(row_power / C + EPS)
    normed = (signal.astype(jnp.float32) * scale[:rows, None] * norm_gain[None, :]).astype(
        jnp.bfloat16
    )
    both = jnp.concatenate([own_half, other_half])
    for d in order[:1]:
        both, taps[d] = tie(both, taps[d])
    half_gain = lax.dynamic_slice_in_dim(norm_gain, core * half, half, 0)
    both = (both.astype(jnp.float32) * scale[:, None] * half_gain[None, :]).astype(jnp.bfloat16)
    blocks = []
    for chunk in range(chunks):
        pieces = [cut(both, chunk * part + (z ^ d) * mine, mine) for d in range(chips)]
        for d in order:
            pieces[d] = along_chips(pieces[d], d)
        blocks.append(pieces)

    width = chunks * mine
    mixed_cores = taps[first]
    swapped = cut(mixed_cores, (1 - core) * width, width)
    taps[first] = jnp.concatenate([cut(mixed_cores, core * width, width), other_core(swapped)])
    fil_spectra = pl.pallas_call(
        functools.partial(spectra_kernel, chips),
        out_shape=[jax.ShapeDtypeStruct((chips, 2 * block, mine), jnp.float32)] * chunks,
        in_specs=[SMEM] + [VMEM] * (2 + chips),
        out_specs=[VMEM] * chunks,
        scratch_shapes=[
            pltpu.VMEM((chips, block, chunks * mine), jnp.bfloat16),
            pltpu.VMEM((chips, 2 * block, chunks * mine), jnp.float32),
        ],
        compiler_params=limits,
        cost_estimate=kernel_cost(),
        name="spectra",
    )(place, fwd_high, fwd_low, *taps)
    *fil_spectra, = tie(*fil_spectra, *blocks[0])
    fil_spectra, blocks[0] = fil_spectra[:chunks], fil_spectra[chunks:]

    results, earlier = [], place
    for chunk in range(chunks):
        pieces = pl.pallas_call(
            functools.partial(convolve_kernel, chips),
            out_shape=[jax.ShapeDtypeStruct((block, mine), jnp.bfloat16)] * chips,
            in_specs=[SMEM, ANY] + [VMEM] * (4 + chips),
            out_specs=[VMEM] * chips,
            scratch_shapes=[
                pltpu.VMEM((chips // pack, block, pack * mine), jnp.bfloat16),
                pltpu.VMEM((chips // pack, 2 * block, pack * mine), jnp.float32),
                pltpu.VMEM((chips // pack, 2 * block, pack * mine), jnp.bfloat16),
                pltpu.VMEM((chips // pack, block, pack * mine), jnp.bfloat16),
            ],
            compiler_params=limits,
            cost_estimate=kernel_cost(),
            name="convolve",
        )(place, earlier, fil_spectra[chunk], fwd_high, fwd_low, inv_high, *blocks[chunk])
        earlier = pieces[0]
        results.append(list(pieces))

    arrived = []
    for chunk, pieces in enumerate(results):
        for d in order:
            pieces[d] = along_chips(pieces[d], d)
        if chunk + 1 < chunks:
            pieces[order[-1]], results[chunk + 1][0] = tie(pieces[order[-1]], results[chunk + 1][0])
        if chunk:
            arrived[0], pieces[order[-1]] = tie(arrived[0], pieces[order[-1]])
        cuts = [lax.dynamic_slice_in_dim(piece, (1 - core) * rows, rows, 0) for piece in pieces]
        arrived += [other_core(jnp.concatenate(cuts)), *pieces]
    skip = skip_gain[None, :]
    if mine % 128 != 0:
        return mix_plain(chips, chunks, z, core, normed, out_gate, skip, arrived)
    return pl.pallas_call(
        functools.partial(mix_kernel, chips, chunks),
        out_shape=jax.ShapeDtypeStruct((rows, channels), jnp.bfloat16),
        in_specs=[SMEM] + [VMEM] * (3 + len(arrived)),
        out_specs=ANY,
        scratch_shapes=[
            pltpu.VMEM((2 * chips * chunks, rows, mine), jnp.bfloat16),
            pltpu.SemaphoreType.DMA((2 * chips * chunks,)),
        ],
        compiler_params=limits,
        cost_estimate=kernel_cost(),
        name="mix",
    )(place, normed, out_gate, skip, *arrived)


def solution(mesh):
    return jax.shard_map(
        local,
        mesh=mesh,
        in_specs=(P("ctx", "ch"), P("ch"), P("ch"), P("ctx", "ch"), P("ctx", "ch")),
        out_specs=P("ctx", "ch"),
        check_vma=False,
    )
```
